32 devices in a mesh: tm: 16 (over z, y, x), tile: 2 (over core).
Axes of the slice: x: 2, y: 2, z: 4, core: 2. Of those that a mesh axis runs over, the one named last changes fastest.
Arguments:
- pivot_inverse: bfloat16 [16, 1024, 1024], P('tm', 'tile'), may hold values from -0.2 to 8.2, as said below
- mult_left: bfloat16 [16, 1024, 1024], P('tm', 'tile'), may hold values from -0.09375 to 0.09375
- mult_right: bfloat16 [16, 1024, 1024], P('tm', 'tile'), may hold values from -0.09375 to 0.09375
- mult_tip: bfloat16 [16, 64, 1024], P('tm', 'tile'), may hold values from -0.09375 to 0.09375
- root_cross: bfloat16 [64, 1024], P(None, 'tile'), may hold values from -0.59765625 to 0.59765625
- root_tip: bfloat16 [64, 64], replicated, may hold values from -0.2 to 8.2, as said below
Outputs:
- marginal_cov: bfloat16 [16, 1024, 1024], P('tm', 'tile')
- cross_cov: bfloat16 [16, 1024, 2048], P('tm', 'tile')
- tip_cov: bfloat16 [16, 64, 1024], P('tm', None, 'tile')
The draws below stay inside these ranges and needn't reach their ends.
Inputs may be any that keep to these rules, and one draw needn't show every extreme that they name: `pivot_inverse`: each of the 16 matrices is symmetric. `root_tip`: symmetric.
All inputs are finite; a program needn't handle non-finite values.
Results may differ from the reference program's by a relative error of at most 0.006.
Values may be sent and summed in bfloat16 or wider, within the bound.
A program may use at most 128 MiB of HBM per device.

```python
import jax
import jax.numpy as jnp
from jax import lax

B = 1024
A = 64
STEPS = 16
LEVELS = 4


def symmetric_draw(key, count, order):
    key_rough, key_main = jax.random.split(key, 2)
    rough = jnp.clip(jax.random.normal(key_rough, (count, order, order), jnp.float32), -4.0, 4.0) * 0.01
    paired = (rough + jnp.swapaxes(rough, 1, 2)) * 0.5
    main = jax.random.uniform(key_main, (count, order), jnp.float32, 0.75, 2.0)
    rows = lax.broadcasted_iota(jnp.int32, (order, order), 0)
    cols = lax.broadcasted_iota(jnp.int32, (order, order), 1)
    unit = (rows == cols).astype(jnp.float32)
    matrix = paired * (1.0 - unit) + unit * main[:, :, None]
    return matrix


def draw_pivot_inverse(key, part):
    return symmetric_draw(jax.random.fold_in(key, 11), STEPS, B).astype(jnp.bfloat16)


def draw_root_tip(key, part):
    return symmetric_draw(jax.random.fold_in(key, 23), 1, A)[0].astype(jnp.bfloat16)


def block_scale(own_key, shape, cuts, low, largest):
    def one(position, parts):
        steps = jax.random.uniform(jax.random.fold_in(jax.random.fold_in(own_key, 6), position), (parts,), jnp.float32, low / len(cuts), largest / len(cuts))
        return jnp.repeat(jnp.exp(steps), shape[position] // parts).reshape((-1,) + (1,) * (len(shape) - position - 1))

    loudness = one(*cuts[0])
    for cut in cuts[1:]:
        loudness = loudness * one(*cut)
    return loudness


def normal_values(rng, extent, width, bound, cuts=(), held_as=jnp.bfloat16):
    array = jax.random.normal(rng, extent, jnp.float32) * width
    if len(cuts) > 0:
        array = block_scale(rng, extent, cuts, -0.22, 0.18) * array
    return jnp.clip(array, min=-bound, max=bound).astype(held_as)


def setup_inputs(seed: int = 0) -> dict:
    key_list = jax.random.split(jax.random.key(seed), 7)
    pivot_inverse = draw_pivot_inverse(jax.random.fold_in(key_list[6], 71), 0)
    mult_left = normal_values(key_list[1], (STEPS, B, B), (4 * B + 2 * A) ** -0.5, 0.09375, ((0, 16), (1, 2)))
    mult_right = normal_values(key_list[2], (STEPS, B, B), (4 * B + 2 * A) ** -0.5, 0.09375, ((0, 16), (1, 2)))
    mult_tip = normal_values(key_list[3], (STEPS, A, B), (4 * B + 2 * A) ** -0.5, 0.09375, ((0, 16), (1, 2)))
    root_cross = normal_values(key_list[4], (A, B), 0.1, 0.59765625, ((1, 2),))
    root_tip = draw_root_tip(jax.random.fold_in(key_list[6], 71), 0)
    return dict(pivot_inverse=pivot_inverse, mult_left=mult_left, mult_right=mult_right, mult_tip=mult_tip, root_cross=root_cross, root_tip=root_tip)


def product(left_matrix, right_matrix):
    return jnp.dot(left_matrix, right_matrix, preferred_element_type=jnp.float32)


def pivots_at(level_index):
    return [block for block in range(STEPS) if block % 2 ** (level_index + 1) == 2 ** level_index - 1]


def reference(pivot_inverse, mult_left, mult_right, mult_tip, root_cross, root_tip):
    offset = 5 % STEPS
    pivot_inverse = jnp.roll(pivot_inverse, offset, axis=0)
    mult_left = jnp.roll(mult_left, offset, axis=0)
    mult_right = jnp.roll(mult_right, offset, axis=0)
    mult_tip = jnp.roll(mult_tip, offset, axis=0)
    last = STEPS - 1
    nodes = pivot_inverse.shape[1]
    zero_block = jnp.zeros((nodes, nodes), jnp.bfloat16)
    zero_tip = jnp.zeros((A, nodes), jnp.bfloat16)
    diagonal = {last: pivot_inverse[last]}
    tip_cross = {last: root_cross}
    self_left = {last: zero_block}
    self_right = {last: zero_block}
    near_left = {last: zero_block}
    near_right = {last: zero_block}
    for level_index in reversed(range(LEVELS)):
        distance = 2 ** level_index
        for block in pivots_at(level_index):
            right_id = block + distance
            left_id = block - distance
            if block >= distance:
                left_diag = diagonal[left_id]
                left_tip = tip_cross[left_id]
                if left_id % 2 ** (level_index + 2) == 2 ** (level_index + 1) - 1:
                    left_right = self_right[left_id]
                    right_left = near_right[left_id]
                else:
                    left_right = near_left[right_id]
                    right_left = self_left[right_id]
            else:
                left_diag = zero_block
                left_tip = zero_tip
                left_right = zero_block
                right_left = zero_block
            g_left = mult_left[block]
            g_right = mult_right[block]
            g_tip = mult_tip[block]
            near_a = product(left_diag, g_left) + product(left_right, g_right) + product(left_tip.T, g_tip)
            near_b = product(right_left, g_left) + product(diagonal[right_id], g_right) + product(tip_cross[right_id].T, g_tip)
            tip_part = product(left_tip, g_left) + product(tip_cross[right_id], g_right) + product(root_tip, g_tip)
            fresh_a = (-near_a).astype(jnp.bfloat16)
            fresh_b = (-near_b).astype(jnp.bfloat16)
            fresh_tip = (-tip_part).astype(jnp.bfloat16)
            own_a = fresh_a.T
            own_b = fresh_b.T
            total = product(own_a, g_left) + product(own_b, g_right) + product(fresh_tip.T, g_tip)
            diagonal[block] = (pivot_inverse[block].astype(jnp.float32) - total).astype(jnp.bfloat16)
            tip_cross[block] = fresh_tip
            near_left[block] = fresh_a
            near_right[block] = fresh_b
            self_left[block] = own_a
            self_right[block] = own_b
    marginal = jnp.stack([diagonal[block_id] for block_id in range(STEPS)])
    crossing = jnp.stack([jnp.concatenate([self_left[block_id], self_right[block_id]], axis=1) for block_id in range(STEPS)])
    tip_blocks = jnp.stack([tip_cross[block_id] for block_id in range(STEPS)])
    marginal = jnp.roll(marginal, -offset, axis=0)
    crossing = jnp.roll(crossing, -offset, axis=0)
    tip_blocks = jnp.roll(tip_blocks, -offset, axis=0)
    return (marginal, crossing, tip_blocks)
```

```python
import jax
import jax.numpy as jnp
from jax import lax
from jax.sharding import PartitionSpec as P


def level_of(block):
    level = 0
    while (block >> level) & 1:
        level += 1
    return level


def dot(left, right, over):
    return lax.dot_general(left, right, ((over[:1], over[1:]), ((), ())), preferred_element_type=jnp.float32)


def body(pivot_inverse, mult_left, mult_right, mult_tip, root_cross, root_tip):
    count = lax.axis_size("tm")
    levels = count.bit_length() - 1
    block = jnp.mod(lax.axis_index("tm") + 5, count)
    half = lax.axis_index("tile")
    rows = pivot_inverse.shape[1]

    def send(shard, pairs):
        return lax.ppermute(shard, "tm", [((s - 5) % count, (t - 5) % count) for s, t in pairs])

    def whole(shard, axis=0):
        return lax.all_gather(shard, "tile", axis=axis, tiled=True)

    low = (block + 1) & -(block + 1)
    right_child = ((((block + 1) // low) >> 1) & 1) == 1
    inverse_rows = pivot_inverse[0]
    full_near = whole(jnp.where(right_child, mult_left[0], mult_right[0]))
    full_far = whole(jnp.where(right_child, mult_right[0], mult_left[0]))
    full_tip = whole(mult_tip[0])
    own_cols = lambda full: lax.dynamic_slice_in_dim(full, half * rows, rows, 1)
    cols_near, cols_far, cols_tip = own_cols(full_near), own_cols(full_far), own_cols(full_tip)
    turn_near, turn_far, turn_tip = cols_near.T, cols_far.T, cols_tip.T
    tip_own = jnp.dot(root_tip, cols_tip, preferred_element_type=jnp.float32)

    is_root = block == count - 1
    diag = jnp.where(is_root, inverse_rows, jnp.zeros_like(inverse_rows))
    tip = jnp.where(is_root, root_cross, jnp.zeros_like(root_cross))
    cross_left = jnp.zeros_like(inverse_rows)
    cross_right = cross_left
    far_ready = None

    def far_of(level):
        distance = 2**level
        pivots = [b for b in range(count) if level_of(b) == level]
        below = [(b - distance, b) for b in pivots if b >= distance and level_of(b - distance) > level + 1]
        above = [(b + distance, b) for b in pivots if level_of(b + distance) > level + 1]
        if not above:
            return None
        got_diag, got_tip = send(diag, above), send(tip, above)
        if below:
            got_diag = jnp.where(right_child, got_diag, send(diag, below))
            got_tip = jnp.where(right_child, got_tip, send(tip, below))
        return whole(got_diag), whole(got_tip, 1)

    for level in reversed(range(levels)):
        distance = 2**level
        pivots = [b for b in range(count) if level_of(b) == level]
        rights = [(b - distance, b) for b in pivots if b >= distance and level_of(b - distance) == level + 1]
        lefts = [(b + distance, b) for b in pivots if level_of(b + distance) == level + 1]
        near_diag, near_tip = send(diag, lefts), send(tip, lefts)
        if rights:
            near_diag = jnp.where(right_child, send(diag, rights), near_diag)
            near_tip = jnp.where(right_child, send(tip, rights), near_tip)
        near_diag, near_tip = whole(near_diag), whole(near_tip, 1)
        far = far_ready
        far_ready = far_of(level - 1) if level >= 1 else None
        part_near = dot(turn_near, near_diag, (1, 1)) + dot(turn_tip, near_tip, (1, 0))
        part_far = None
        part_tip = jnp.dot(near_tip, cols_near, preferred_element_type=jnp.float32) + tip_own
        if far is not None:
            far_diag, far_tip = far
            between = send(cross_left, [p for p in lefts if p[0] != count - 1])
            between = jnp.where(right_child, send(cross_right, rights), between)
            between = whole(between)
            part_near = part_near + dot(turn_far, between, (1, 1))
            part_far = (
                dot(turn_far, far_diag, (1, 1))
                + dot(turn_tip, far_tip, (1, 0))
                + dot(turn_near, between, (1, 0))
            )
            part_tip = part_tip + jnp.dot(far_tip, cols_far, preferred_element_type=jnp.float32)
        fresh_near = (-part_near).astype(jnp.bfloat16)
        fresh_tip = (-part_tip).astype(jnp.bfloat16)
        total = dot(fresh_near, full_near, (1, 0)) + dot(fresh_tip, full_tip, (0, 0))
        if part_far is not None:
            fresh_far = (-part_far).astype(jnp.bfloat16)
            total = total + dot(fresh_far, full_far, (1, 0))
        else:
            fresh_far = jnp.zeros_like(fresh_near)
        if far is not None:
            exists = right_child | (block >= distance)
            fresh_far = jnp.where(exists, fresh_far, jnp.zeros_like(fresh_far))
        fresh_diag = (inverse_rows.astype(jnp.float32) - total).astype(jnp.bfloat16)
        active = jnp.mod(block, 2 ** (level + 1)) == distance - 1
        diag = jnp.where(active, fresh_diag, diag)
        tip = jnp.where(active, fresh_tip, tip)
        cross_left = jnp.where(active, jnp.where(right_child, fresh_near, fresh_far), cross_left)
        cross_right = jnp.where(active, jnp.where(right_child, fresh_far, fresh_near), cross_right)
    crossing = jnp.concatenate([cross_left, cross_right], axis=1)
    return (diag[None], crossing[None], tip[None])


def solution(mesh):
    placed = (
        P("tm", "tile", None),
        P("tm", "tile", None),
        P("tm", "tile", None),
        P("tm", "tile", None),
        P(None, "tile"),
        P(),
    )
    return jax.shard_map(
        body,
        mesh=mesh,
        in_specs=placed,
        out_specs=(P("tm", "tile", None), P("tm", "tile", None), P("tm", None, "tile")),
        check_vma=False,
    )
```

```python
import jax
import jax.numpy as jnp
from jax import lax
from jax.sharding import PartitionSpec as P


def level_of(block):
    level = 0
    while (block >> level) & 1:
        level += 1
    return level


def dot(left, right, over):
    return lax.dot_general(left, right, ((over[:1], over[1:]), ((), ())), preferred_element_type=jnp.float32)


def body(pivot_inverse, mult_left, mult_right, mult_tip, root_cross, root_tip):
    count = lax.axis_size("tm")
    levels = count.bit_length() - 1
    block = jnp.mod(lax.axis_index("tm") + 5, count)
    half = lax.axis_index("tile")
    rows = pivot_inverse.shape[1]

    def send(shard, pairs):
        return lax.ppermute(shard, "tm", [((s - 5) % count, (t - 5) % count) for s, t in pairs])

    def detour(shard, pairs, via):
        row = lambda b: (b - 5) % count
        first = [(row(s), via(row(s), row(t))) for s, t in pairs]
        last = [(f[1], row(t)) for f, (_, t) in zip(first, pairs)]
        distinct = len({f[1] for f in first}) == len(first)
        if not distinct or any(a == b for a, b in first + last):
            return send(shard, pairs)
        return lax.ppermute(lax.ppermute(shard, "tm", first), "tm", last)

    def whole(shard, axis=0):
        return lax.all_gather(shard, "tile", axis=axis, tiled=True)

    low = (block + 1) & -(block + 1)
    right_child = ((((block + 1) // low) >> 1) & 1) == 1
    inverse_rows = pivot_inverse[0]
    full_near = whole(jnp.where(right_child, mult_left[0], mult_right[0]))
    full_far = whole(jnp.where(right_child, mult_right[0], mult_left[0]))
    full_tip = whole(mult_tip[0])
    own_cols = lambda full: lax.dynamic_slice_in_dim(full, half * rows, rows, 1)
    cols_near, cols_far, cols_tip = own_cols(full_near), own_cols(full_far), own_cols(full_tip)
    turn_near, turn_far, turn_tip = cols_near.T, cols_far.T, cols_tip.T
    tip_own = jnp.dot(root_tip, cols_tip, preferred_element_type=jnp.float32)

    is_root = block == count - 1
    diag = jnp.where(is_root, inverse_rows, jnp.zeros_like(inverse_rows))
    tip = jnp.where(is_root, root_cross, jnp.zeros_like(root_cross))
    cross_left = jnp.zeros_like(inverse_rows)
    cross_right = cross_left
    far_ready = None

    def far_of(level, diag, tip):
        distance = 2**level
        pivots = [b for b in range(count) if level_of(b) == level]
        below = [(b - distance, b) for b in pivots if b >= distance and level_of(b - distance) > level + 1]
        above = [(b + distance, b) for b in pivots if level_of(b + distance) > level + 1]
        if not above:
            return None
        got = [send(diag, above), send(tip, above)]
        if below:
            got += [send(diag, below), send(tip, below)]
        return tuple(got)

    def far_whole(got):
        got_diag, got_tip = got[:2]
        if len(got) == 4:
            got_diag = jnp.where(right_child, got_diag, got[2])
            got_tip = jnp.where(right_child, got_tip, got[3])
        return whole(got_diag), whole(got_tip, 1)

    for level in reversed(range(levels)):
        distance = 2**level
        pivots = [b for b in range(count) if level_of(b) == level]
        rights = [(b - distance, b) for b in pivots if b >= distance and level_of(b - distance) == level + 1]
        lefts = [(b + distance, b) for b in pivots if level_of(b + distance) == level + 1]
        send_left, send_right = send, send
        if level == 0:
            send_left = lambda shard, pairs: detour(shard, pairs, lambda s, t: s ^ 2)
        if level == 1:
            send_right = lambda shard, pairs: detour(shard, pairs, lambda s, t: (t & ~3) | (s & 3))
        near_tip = send(tip, lefts)
        if rights:
            near_tip = jnp.where(right_child, send(tip, rights), near_tip)
        near_diag = send_left(diag, lefts)
        if rights:
            near_diag = jnp.where(right_child, send_right(diag, rights), near_diag)
        between = None
        if rights:
            crossed = [p for p in lefts if p[0] != count - 1 and p[1] >= distance]
            between = send_right(cross_right, rights)
            if crossed:
                between = jnp.where(right_child, between, send_left(cross_left, crossed))
        far = far_ready
        far_ready = None
        if level >= 1:
            arrived = near_diag if between is None else (near_diag, between)
            arrived, late_diag, late_tip = lax.optimization_barrier((arrived, diag, tip))
            near_diag, between = (arrived, None) if between is None else arrived
            far_ready = far_of(level - 1, late_diag, late_tip)
        near_diag, near_tip = whole(near_diag), whole(near_tip, 1)
        part_near = dot(turn_near, near_diag, (1, 1)) + dot(turn_tip, near_tip, (1, 0))
        part_far = None
        part_tip = jnp.dot(near_tip, cols_near, preferred_element_type=jnp.float32) + tip_own
        if far is not None:
            far_diag, far_tip = far
            between = whole(between)
            part_near = part_near + dot(turn_far, between, (1, 1))
            part_far = (
                dot(turn_far, far_diag, (1, 1))
                + dot(turn_tip, far_tip, (1, 0))
                + dot(turn_near, between, (1, 0))
            )
            part_tip = part_tip + jnp.dot(far_tip, cols_far, preferred_element_type=jnp.float32)
        fresh_near = (-part_near).astype(jnp.bfloat16)
        fresh_tip = (-part_tip).astype(jnp.bfloat16)
        total = dot(fresh_near, full_near, (1, 0)) + dot(fresh_tip, full_tip, (0, 0))
        if part_far is not None:
            fresh_far = (-part_far).astype(jnp.bfloat16)
            total = total + dot(fresh_far, full_far, (1, 0))
        else:
            fresh_far = jnp.zeros_like(fresh_near)
        if far is not None:
            exists = right_child | (block >= distance)
            fresh_far = jnp.where(exists, fresh_far, jnp.zeros_like(fresh_far))
        fresh_diag = (inverse_rows.astype(jnp.float32) - total).astype(jnp.bfloat16)
        if far_ready is not None:
            fresh_diag, far_ready = lax.optimization_barrier((fresh_diag, far_ready))
            far_ready = far_whole(far_ready)
        active = jnp.mod(block, 2 ** (level + 1)) == distance - 1
        diag = jnp.where(active, fresh_diag, diag)
        tip = jnp.where(active, fresh_tip, tip)
        cross_left = jnp.where(active, jnp.where(right_child, fresh_near, fresh_far), cross_left)
        cross_right = jnp.where(active, jnp.where(right_child, fresh_far, fresh_near), cross_right)
    crossing = jnp.concatenate([cross_left, cross_right], axis=1)
    return (diag[None], crossing[None], tip[None])


def solution(mesh):
    placed = (
        P("tm", "tile", None),
        P("tm", "tile", None),
        P("tm", "tile", None),
        P("tm", "tile", None),
        P(None, "tile"),
        P(),
    )
    return jax.shard_map(
        body,
        mesh=mesh,
        in_specs=placed,
        out_specs=(P("tm", "tile", None), P("tm", "tile", None), P("tm", None, "tile")),
        check_vma=False,
    )
```

```python
import jax
import jax.numpy as jnp
from jax import lax
from jax.sharding import PartitionSpec as P


def level_of(block):
    level = 0
    while (block >> level) & 1:
        level += 1
    return level


def dot(left, right, over):
    return lax.dot_general(left, right, ((over[:1], over[1:]), ((), ())), preferred_element_type=jnp.float32)


def body(pivot_inverse, mult_left, mult_right, mult_tip, root_cross, root_tip):
    count = lax.axis_size("tm")
    levels = count.bit_length() - 1
    block = jnp.mod(lax.axis_index("tm") + 5, count)
    half = lax.axis_index("tile")
    rows = pivot_inverse.shape[1]

    def send(shard, pairs):
        return lax.ppermute(shard, "tm", [((s - 5) % count, (t - 5) % count) for s, t in pairs])

    def detour(shard, pairs, via):
        row = lambda b: (b - 5) % count
        first = [(row(s), via(row(s), row(t))) for s, t in pairs]
        last = [(f[1], row(t)) for f, (_, t) in zip(first, pairs)]
        distinct = len({f[1] for f in first}) == len(first)
        if not distinct or any(a == b for a, b in first + last):
            return send(shard, pairs)
        return lax.ppermute(lax.ppermute(shard, "tm", first), "tm", last)

    def whole(shard, axis=0):
        other = lax.ppermute(shard, "tile", [(0, 1), (1, 0)])
        first = half == 0
        return jnp.concatenate([jnp.where(first, shard, other), jnp.where(first, other, shard)], axis=axis)

    low = (block + 1) & -(block + 1)
    right_child = ((((block + 1) // low) >> 1) & 1) == 1
    inverse_rows = pivot_inverse[0]
    full_near = whole(jnp.where(right_child, mult_left[0], mult_right[0]))
    full_far = whole(jnp.where(right_child, mult_right[0], mult_left[0]))
    full_tip = whole(mult_tip[0])
    own_cols = lambda full: lax.dynamic_slice_in_dim(full, half * rows, rows, 1)
    cols_near, cols_far, cols_tip = own_cols(full_near), own_cols(full_far), own_cols(full_tip)
    turn_near, turn_far, turn_tip = cols_near.T, cols_far.T, cols_tip.T
    tip_own = jnp.dot(root_tip, cols_tip, preferred_element_type=jnp.float32)

    is_root = block == count - 1
    diag = jnp.where(is_root, inverse_rows, jnp.zeros_like(inverse_rows))
    tip = jnp.where(is_root, root_cross, jnp.zeros_like(root_cross))
    cross_left = jnp.zeros_like(inverse_rows)
    cross_right = cross_left
    far_ready = None

    def far_of(level, diag, tip):
        distance = 2**level
        pivots = [b for b in range(count) if level_of(b) == level]
        below = [(b - distance, b) for b in pivots if b >= distance and level_of(b - distance) > level + 1]
        above = [(b + distance, b) for b in pivots if level_of(b + distance) > level + 1]
        if not above:
            return None
        got = [send(diag, above), send(tip, above)]
        if below:
            got += [send(diag, below), send(tip, below)]
        return tuple(got)

    def far_whole(got):
        got_diag, got_tip = got[:2]
        if len(got) == 4:
            got_diag = jnp.where(right_child, got_diag, got[2])
            got_tip = jnp.where(right_child, got_tip, got[3])
        return whole(got_diag), whole(got_tip, 1)

    for level in reversed(range(levels)):
        distance = 2**level
        pivots = [b for b in range(count) if level_of(b) == level]
        rights = [(b - distance, b) for b in pivots if b >= distance and level_of(b - distance) == level + 1]
        lefts = [(b + distance, b) for b in pivots if level_of(b + distance) == level + 1]
        send_left, send_right = send, send
        if level == 0:
            send_left = lambda shard, pairs: detour(shard, pairs, lambda s, t: s ^ 2)
        if level == 1:
            send_right = lambda shard, pairs: detour(shard, pairs, lambda s, t: (t & ~3) | (s & 3))
        near_tip = send(tip, lefts)
        if rights:
            near_tip = jnp.where(right_child, send(tip, rights), near_tip)
        near_diag = send_left(diag, lefts)
        if rights:
            near_diag = jnp.where(right_child, send_right(diag, rights), near_diag)
        between = None
        if rights:
            crossed = [p for p in lefts if p[0] != count - 1 and p[1] >= distance]
            between = send_right(cross_right, rights)
            if crossed:
                between = jnp.where(right_child, between, send_left(cross_left, crossed))
        far = far_ready
        far_ready = None
        if level >= 1:
            arrived = near_diag if between is None else (near_diag, between)
            arrived, late_diag, late_tip = lax.optimization_barrier((arrived, diag, tip))
            near_diag, between = (arrived, None) if between is None else arrived
            far_ready = far_of(level - 1, late_diag, late_tip)
        near_diag, near_tip = whole(near_diag), whole(near_tip, 1)
        part_near = dot(turn_near, near_diag, (1, 1)) + dot(turn_tip, near_tip, (1, 0))
        part_far = None
        part_tip = jnp.dot(near_tip, cols_near, preferred_element_type=jnp.float32) + tip_own
        if far is not None:
            far_diag, far_tip = far
            between = whole(between)
            part_near = part_near + dot(turn_far, between, (1, 1))
            part_far = (
                dot(turn_far, far_diag, (1, 1))
                + dot(turn_tip, far_tip, (1, 0))
                + dot(turn_near, between, (1, 0))
            )
            part_tip = part_tip + jnp.dot(far_tip, cols_far, preferred_element_type=jnp.float32)
        fresh_near = (-part_near).astype(jnp.bfloat16)
        fresh_tip = (-part_tip).astype(jnp.bfloat16)
        total = dot(fresh_near, full_near, (1, 0)) + dot(fresh_tip, full_tip, (0, 0))
        if part_far is not None:
            fresh_far = (-part_far).astype(jnp.bfloat16)
            total = total + dot(fresh_far, full_far, (1, 0))
        else:
            fresh_far = jnp.zeros_like(fresh_near)
        if far is not None:
            exists = right_child | (block >= distance)
            fresh_far = jnp.where(exists, fresh_far, jnp.zeros_like(fresh_far))
        fresh_diag = (inverse_rows.astype(jnp.float32) - total).astype(jnp.bfloat16)
        if far_ready is not None:
            fresh_diag, far_ready = lax.optimization_barrier((fresh_diag, far_ready))
            far_ready = far_whole(far_ready)
        active = jnp.mod(block, 2 ** (level + 1)) == distance - 1
        diag = jnp.where(active, fresh_diag, diag)
        tip = jnp.where(active, fresh_tip, tip)
        cross_left = jnp.where(active, jnp.where(right_child, fresh_near, fresh_far), cross_left)
        cross_right = jnp.where(active, jnp.where(right_child, fresh_far, fresh_near), cross_right)
    crossing = jnp.concatenate([cross_left, cross_right], axis=1)
    return (diag[None], crossing[None], tip[None])


def solution(mesh):
    placed = (
        P("tm", "tile", None),
        P("tm", "tile", None),
        P("tm", "tile", None),
        P("tm", "tile", None),
        P(None, "tile"),
        P(),
    )
    return jax.shard_map(
        body,
        mesh=mesh,
        in_specs=placed,
        out_specs=(P("tm", "tile", None), P("tm", "tile", None), P("tm", None, "tile")),
        check_vma=False,
    )
```

```python
import jax
import jax.numpy as jnp
from jax import lax
from jax.sharding import PartitionSpec as P


def level_of(block):
    level = 0
    while (block >> level) & 1:
        level += 1
    return level


def dot(left, right, over):
    return lax.dot_general(left, right, ((over[:1], over[1:]), ((), ())), preferred_element_type=jnp.float32)


def body(pivot_inverse, mult_left, mult_right, mult_tip, root_cross, root_tip):
    count = lax.axis_size("tm")
    levels = count.bit_length() - 1
    block = jnp.mod(lax.axis_index("tm") + 5, count)
    half = lax.axis_index("tile")
    rows = pivot_inverse.shape[1]

    def send(shard, pairs):
        return lax.ppermute(shard, "tm", [((s - 5) % count, (t - 5) % count) for s, t in pairs])

    def detour(shard, pairs, via):
        row = lambda b: (b - 5) % count
        first = [(row(s), via(row(s), row(t))) for s, t in pairs]
        last = [(f[1], row(t)) for f, (_, t) in zip(first, pairs)]
        distinct = len({f[1] for f in first}) == len(first)
        if not distinct or any(a == b for a, b in first + last):
            return send(shard, pairs)
        return lax.ppermute(lax.ppermute(shard, "tm", first), "tm", last)

    def whole(shard, axis=0):
        other = lax.ppermute(shard, "tile", [(0, 1), (1, 0)])
        first = half == 0
        return jnp.concatenate([jnp.where(first, shard, other), jnp.where(first, other, shard)], axis=axis)

    low = (block + 1) & -(block + 1)
    right_child = ((((block + 1) // low) >> 1) & 1) == 1
    inverse_rows = pivot_inverse[0]
    full_near = whole(jnp.where(right_child, mult_left[0], mult_right[0]))
    full_far = whole(jnp.where(right_child, mult_right[0], mult_left[0]))
    full_tip = whole(mult_tip[0])
    own_cols = lambda full: lax.dynamic_slice_in_dim(full, half * rows, rows, 1)
    cols_near, cols_far, cols_tip = own_cols(full_near), own_cols(full_far), own_cols(full_tip)
    turn_near, turn_far, turn_tip = cols_near.T, cols_far.T, cols_tip.T
    tip_own = jnp.dot(root_tip, cols_tip, preferred_element_type=jnp.float32)

    is_root = block == count - 1
    diag = jnp.where(is_root, inverse_rows, jnp.zeros_like(inverse_rows))
    tip = jnp.where(is_root, root_cross, jnp.zeros_like(root_cross))
    cross_left = jnp.zeros_like(inverse_rows)
    cross_right = cross_left
    far_ready = None

    def far_of(level, diag, tip):
        distance = 2**level
        pivots = [b for b in range(count) if level_of(b) == level]
        below = [(b - distance, b) for b in pivots if b >= distance and level_of(b - distance) > level + 1]
        above = [(b + distance, b) for b in pivots if level_of(b + distance) > level + 1]
        if not above:
            return None
        got = [send(diag, above), send(tip, above)]
        if below:
            got += [send(diag, below), send(tip, below)]
        return tuple(got)

    def far_whole(got):
        got_diag, got_tip = got[:2]
        if len(got) == 4:
            got_diag = jnp.where(right_child, got_diag, got[2])
            got_tip = jnp.where(right_child, got_tip, got[3])
        return whole(got_diag), whole(got_tip, 1)

    for level in reversed(range(levels)):
        distance = 2**level
        pivots = [b for b in range(count) if level_of(b) == level]
        rights = [(b - distance, b) for b in pivots if b >= distance and level_of(b - distance) == level + 1]
        lefts = [(b + distance, b) for b in pivots if level_of(b + distance) == level + 1]
        send_left, send_right = send, send
        if level == 0:
            send_left = lambda shard, pairs: detour(shard, pairs, lambda s, t: s ^ 2)
        if level == 2:
            send_left = lambda shard, pairs: detour(shard, pairs, lambda s, t: t ^ 1)
        if level == 1:
            send_right = lambda shard, pairs: detour(shard, pairs, lambda s, t: (t & ~3) | (s & 3))
        near_tip = send(tip, lefts)
        if rights:
            near_tip = jnp.where(right_child, send(tip, rights), near_tip)
        near_diag = send_left(diag, lefts)
        if rights:
            near_diag = jnp.where(right_child, send_right(diag, rights), near_diag)
        between = None
        if rights:
            crossed = [p for p in lefts if p[0] != count - 1 and p[1] >= distance]
            between = send_right(cross_right, rights)
            if crossed:
                between = jnp.where(right_child, between, send_left(cross_left, crossed))
        far = far_ready
        far_ready = None
        if level >= 1:
            arrived = near_diag if between is None else (near_diag, between)
            arrived, late_diag, late_tip = lax.optimization_barrier((arrived, diag, tip))
            near_diag, between = (arrived, None) if between is None else arrived
            far_ready = far_of(level - 1, late_diag, late_tip)
        near_diag, near_tip = whole(near_diag), whole(near_tip, 1)
        part_near = dot(turn_near, near_diag, (1, 1)) + dot(turn_tip, near_tip, (1, 0))
        part_far = None
        part_tip = jnp.dot(near_tip, cols_near, preferred_element_type=jnp.float32) + tip_own
        if far is not None:
            far_diag, far_tip = far
            between = whole(between)
            part_near = part_near + dot(turn_far, between, (1, 1))
            part_far = (
                dot(turn_far, far_diag, (1, 1))
                + dot(turn_tip, far_tip, (1, 0))
                + dot(turn_near, between, (1, 0))
            )
            part_tip = part_tip + jnp.dot(far_tip, cols_far, preferred_element_type=jnp.float32)
        fresh_near = (-part_near).astype(jnp.bfloat16)
        fresh_tip = (-part_tip).astype(jnp.bfloat16)
        total = dot(fresh_near, full_near, (1, 0)) + dot(fresh_tip, full_tip, (0, 0))
        if part_far is not None:
            fresh_far = (-part_far).astype(jnp.bfloat16)
            total = total + dot(fresh_far, full_far, (1, 0))
        else:
            fresh_far = jnp.zeros_like(fresh_near)
        if far is not None:
            exists = right_child | (block >= distance)
            fresh_far = jnp.where(exists, fresh_far, jnp.zeros_like(fresh_far))
        fresh_diag = (inverse_rows.astype(jnp.float32) - total).astype(jnp.bfloat16)
        if far_ready is not None:
            fresh_diag, far_ready = lax.optimization_barrier((fresh_diag, far_ready))
            far_ready = far_whole(far_ready)
        active = jnp.mod(block, 2 ** (level + 1)) == distance - 1
        diag = jnp.where(active, fresh_diag, diag)
        tip = jnp.where(active, fresh_tip, tip)
        cross_left = jnp.where(active, jnp.where(right_child, fresh_near, fresh_far), cross_left)
        cross_right = jnp.where(active, jnp.where(right_child, fresh_far, fresh_near), cross_right)
    crossing = jnp.concatenate([cross_left, cross_right], axis=1)
    return (diag[None], crossing[None], tip[None])


def solution(mesh):
    placed = (
        P("tm", "tile", None),
        P("tm", "tile", None),
        P("tm", "tile", None),
        P("tm", "tile", None),
        P(None, "tile"),
        P(),
    )
    return jax.shard_map(
        body,
        mesh=mesh,
        in_specs=placed,
        out_specs=(P("tm", "tile", None), P("tm", "tile", None), P("tm", None, "tile")),
        check_vma=False,
    )
```

```python
import jax
import jax.numpy as jnp
from jax import lax
from jax.sharding import PartitionSpec as P


def level_of(block):
    level = 0
    while (block >> level) & 1:
        level += 1
    return level


def dot(left, right, over):
    return lax.dot_general(left, right, ((over[:1], over[1:]), ((), ())), preferred_element_type=jnp.float32)


def body(pivot_inverse, mult_left, mult_right, mult_tip, root_cross, root_tip):
    count = lax.axis_size("tm")
    levels = count.bit_length() - 1
    block = jnp.mod(lax.axis_index("tm") + 5, count)
    half = lax.axis_index("tile")
    rows = pivot_inverse.shape[1]

    def send(shard, pairs):
        return lax.ppermute(shard, "tm", [((s - 5) % count, (t - 5) % count) for s, t in pairs])

    def detour(shard, pairs, via):
        row = lambda b: (b - 5) % count
        first = [(row(s), via(row(s), row(t))) for s, t in pairs]
        last = [(f[1], row(t)) for f, (_, t) in zip(first, pairs)]
        distinct = len({f[1] for f in first}) == len(first)
        if not distinct or any(a == b for a, b in first + last):
            return send(shard, pairs)
        return lax.ppermute(lax.ppermute(shard, "tm", first), "tm", last)

    def whole(shard, axis=0):
        other = lax.ppermute(shard, "tile", [(0, 1), (1, 0)])
        first = half == 0
        return jnp.concatenate([jnp.where(first, shard, other), jnp.where(first, other, shard)], axis=axis)

    low = (block + 1) & -(block + 1)
    right_child = ((((block + 1) // low) >> 1) & 1) == 1
    inverse_rows = pivot_inverse[0]
    full_near = whole(jnp.where(right_child, mult_left[0], mult_right[0]))
    full_far = whole(jnp.where(right_child, mult_right[0], mult_left[0]))
    full_tip = whole(mult_tip[0])
    own_cols = lambda full: lax.dynamic_slice_in_dim(full, half * rows, rows, 1)
    cols_near, cols_far, cols_tip = own_cols(full_near), own_cols(full_far), own_cols(full_tip)
    turn_near, turn_far, turn_tip = cols_near.T, cols_far.T, cols_tip.T
    tip_own = jnp.dot(root_tip, cols_tip, preferred_element_type=jnp.float32)

    is_root = block == count - 1
    diag = jnp.where(is_root, inverse_rows, jnp.zeros_like(inverse_rows))
    tip = jnp.where(is_root, root_cross, jnp.zeros_like(root_cross))
    cross_left = jnp.zeros_like(inverse_rows)
    cross_right = cross_left
    far_ready = None

    def far_of(level, diag, tip):
        distance = 2**level
        pivots = [b for b in range(count) if level_of(b) == level]
        below = [(b - distance, b) for b in pivots if b >= distance and level_of(b - distance) > level + 1]
        above = [(b + distance, b) for b in pivots if level_of(b + distance) > level + 1]
        if not above:
            return None
        got = [send(diag, above), send(tip, above)]
        if below:
            got += [send(diag, below), send(tip, below)]
        return tuple(got)

    def far_whole(got):
        got_diag, got_tip = got[:2]
        if len(got) == 4:
            got_diag = jnp.where(right_child, got_diag, got[2])
            got_tip = jnp.where(right_child, got_tip, got[3])
        return whole(got_diag), whole(got_tip, 1)

    for level in reversed(range(levels)):
        distance = 2**level
        pivots = [b for b in range(count) if level_of(b) == level]
        rights = [(b - distance, b) for b in pivots if b >= distance and level_of(b - distance) == level + 1]
        lefts = [(b + distance, b) for b in pivots if level_of(b + distance) == level + 1]
        send_left, send_right = send, send
        if level == 0:
            send_left = lambda shard, pairs: detour(shard, pairs, lambda s, t: s ^ 2)
        if level == 2:
            send_left = lambda shard, pairs: detour(shard, pairs, lambda s, t: t ^ 1)
        if level == 1:
            send_right = lambda shard, pairs: detour(shard, pairs, lambda s, t: (t & ~3) | (s & 3))
        near_tip = send(tip, lefts)
        if rights:
            near_tip = jnp.where(right_child, send(tip, rights), near_tip)
        near_diag = send_left(diag, lefts)
        if rights:
            near_diag = jnp.where(right_child, send_right(diag, rights), near_diag)
        between = None
        if rights:
            crossed = [p for p in lefts if p[0] != count - 1 and p[1] >= distance]
            between = send_right(cross_right, rights)
            if crossed:
                between = jnp.where(right_child, between, send_left(cross_left, crossed))
        far = far_ready
        far_ready = None
        if level >= 1:
            arrived = near_diag if between is None else (near_diag, between)
            arrived, late_diag, late_tip = lax.optimization_barrier((arrived, diag, tip))
            near_diag, between = (arrived, None) if between is None else arrived
            far_ready = far_of(level - 1, late_diag, late_tip)
        near_diag, near_tip = whole(near_diag), whole(near_tip, 1)
        part_near = dot(turn_near, near_diag, (1, 1)) + dot(turn_tip, near_tip, (1, 0))
        part_far = None
        part_tip = jnp.dot(near_tip, cols_near, preferred_element_type=jnp.float32) + tip_own
        if far is not None:
            far_diag, far_tip = far
            between = whole(between)
            part_near = part_near + dot(turn_far, between, (1, 1))
            part_far = (
                dot(turn_far, far_diag, (1, 1))
                + dot(turn_tip, far_tip, (1, 0))
                + dot(turn_near, between, (1, 0))
            )
            part_tip = part_tip + jnp.dot(far_tip, cols_far, preferred_element_type=jnp.float32)
        fresh_near = (-part_near).astype(jnp.bfloat16)
        fresh_tip = (-part_tip).astype(jnp.bfloat16)
        total = dot(fresh_near, full_near, (1, 0)) + dot(fresh_tip, full_tip, (0, 0))
        if part_far is not None:
            fresh_far = (-part_far).astype(jnp.bfloat16)
            total = total + dot(fresh_far, full_far, (1, 0))
        else:
            fresh_far = jnp.zeros_like(fresh_near)
        if far is not None:
            exists = right_child | (block >= distance)
            fresh_far = jnp.where(exists, fresh_far, jnp.zeros_like(fresh_far))
        fresh_diag = (inverse_rows.astype(jnp.float32) - total).astype(jnp.bfloat16)
        if far_ready is not None:
            _, far_ready = lax.optimization_barrier((fresh_diag, far_ready))
            far_ready = far_whole(far_ready)
        active = jnp.mod(block, 2 ** (level + 1)) == distance - 1
        diag = jnp.where(active, fresh_diag, diag)
        tip = jnp.where(active, fresh_tip, tip)
        cross_left = jnp.where(active, jnp.where(right_child, fresh_near, fresh_far), cross_left)
        cross_right = jnp.where(active, jnp.where(right_child, fresh_far, fresh_near), cross_right)
    crossing = jnp.concatenate([cross_left, cross_right], axis=1)
    return (diag[None], crossing[None], tip[None])


def solution(mesh):
    placed = (
        P("tm", "tile", None),
        P("tm", "tile", None),
        P("tm", "tile", None),
        P("tm", "tile", None),
        P(None, "tile"),
        P(),
    )
    return jax.shard_map(
        body,
        mesh=mesh,
        in_specs=placed,
        out_specs=(P("tm", "tile", None), P("tm", "tile", None), P("tm", None, "tile")),
        check_vma=False,
    )
```
